128 devices in a mesh: lon: 8 (over y_hi, x), lat: 16 (over y_lo, z, core).
Axes of the slice: x: 4, y: 4 (y_hi: 2, y_lo: 2; y = y_hi * 2 + y_lo), z: 4, core: 2. Of those that a mesh axis runs over, the one named last changes fastest.
Arguments:
- probe: float32 [32, 720, 1440], P(None, 'lat', 'lon'), may hold values from -6 to 6
- residual: float32 [32, 720, 1440], P(None, 'lat', 'lon'), may hold values from -6 to 6
- lon_embed: float32 [1440, 16], replicated, may hold values from -6 to 6
- lat_embed: float32 [720, 16], replicated, may hold values from -6 to 6
- day_embed: float32 [32, 16], replicated, may hold values from -6 to 6
- scales: float32 [3], replicated, may hold values from 3 to 6
Outputs:
- products: float32 [2, 4, 32, 720, 1440], P(None, None, 'lat', 'lon')
The draws below stay inside these ranges and needn't reach their ends.
All inputs are finite; a program needn't handle non-finite values.
Results may differ from the reference program's by a relative error of at most 0.00014.
Values sent between devices are 32-bit elements; how exact they have to be, the bound alone decides.
No kernel may reach another device: no remote copies, remote signals or barrier semaphores. Data moves between devices by JAX's collectives and lax.ppermute only.
A program may use at most 128 MiB of HBM per device.

```python
import math
import jax
import jax.numpy as jnp
from jax import lax

NL = 1440
NA = 720
ND = 32
EMB = 16


def level_of(rng, dims, cuts, smallest, largest):
    gain, own = 1.0, jax.random.fold_in(rng, 6)
    for axis_at, parts in cuts:
        steps = jnp.exp(jax.random.uniform(jax.random.fold_in(own, axis_at), (parts,), jnp.float32, smallest / len(cuts), largest / len(cuts)))
        gain = gain * jnp.repeat(steps, dims[axis_at] // parts).reshape([-1 if axis == axis_at else 1 for axis in range(len(dims))])
    return gain


def centred(key, shape, scale, most, shards=(), dtype=jnp.bfloat16):
    result = scale * jax.random.normal(key, shape, jnp.float32)
    if shards:
        result = result * level_of(key, shape, shards, -0.22, 0.18)
    return jnp.clip(result, -most, most).astype(dtype)


def setup_inputs(seed: int = 0) -> dict:
    key_of = jax.random.split(jax.random.key(seed), 7)
    return {
        "probe": centred(key_of[0], (ND, NA, NL), 1.0, 6.0, ((1, 16), (2, 8)), jnp.float32),
        "residual": centred(key_of[1], (ND, NA, NL), 1.0, 6.0, ((1, 16), (2, 8)), jnp.float32),
        "lon_embed": centred(key_of[2], (NL, EMB), 1.0, 6.0, (), jnp.float32),
        "lat_embed": centred(key_of[3], (NA, EMB), 1.0, 6.0, (), jnp.float32),
        "day_embed": centred(key_of[4], (ND, EMB), 1.0, 6.0, (), jnp.float32),
        "scales": jnp.clip(jnp.exp(jax.random.uniform(key_of[5], (3,), jnp.float32, math.log(3.0), math.log(6.0))), 3.0, 6.0),
    }


def factors(embed, scale):
    count = embed.shape[0]
    squares = lax.optimization_barrier(jnp.sum(embed * embed, axis=1))
    inner = jnp.dot(embed, embed.T, precision=lax.Precision.HIGHEST, preferred_element_type=jnp.float32)
    dist = squares[:, None] + squares[None, :] - 2.0 * inner
    kern = jnp.exp(-dist / (2.0 * scale * scale)) / math.sqrt(count)
    deriv = kern * dist / (scale * scale * scale)
    return (kern, deriv)

def along_day(field, mat):
    return jnp.einsum('dal,de->eal', field, mat, precision=lax.Precision.HIGHEST)

def along_lat(field, mat):
    return jnp.einsum('dal,ae->del', field, mat, precision=lax.Precision.HIGHEST)

def along_lon(field, mat):
    return jnp.einsum('dal,lm->dam', field, mat, precision=lax.Precision.HIGHEST)

def reference(probe, residual, lon_embed, lat_embed, day_embed, scales):
    lon_k, lon_g = factors(lon_embed, scales[0])
    lat_k, lat_g = factors(lat_embed, scales[1])
    day_k, day_g = factors(day_embed, scales[2])
    results = []
    for field in (probe, residual):
        plain = along_day(field, day_k)
        day_part = along_day(field, day_g)
        both = along_lat(plain, lat_k)
        base = along_lon(both, lon_k)
        by_day = along_lon(along_lat(day_part, lat_k), lon_k)
        by_lon = along_lon(both, lon_g)
        by_lat = along_lon(along_lat(plain, lat_g), lon_k)
        results.append(jnp.stack([base, by_day, by_lon, by_lat]))
    return jnp.stack(results)
```

```python
import functools
import math

import jax
import jax.numpy as jnp
from jax import lax
from jax.experimental import pallas as pl
from jax.experimental.pallas import tpu as pltpu
from jax.sharding import PartitionSpec as P

NL = 1440
NA = 720
ND = 32
F32 = jnp.float32
BF16 = jnp.bfloat16
VMEM_LIMIT = 56 * 1024 * 1024

LOCAL_LON = 180
REST = LOCAL_LON - 128
LATS = 45
SLOTS = 46
DAY_ROWS = SLOTS * 12
OUT_LATS = 90
LAT_ROWS = 544


def params(**kw):
    return pltpu.CompilerParams(vmem_limit_bytes=VMEM_LIMIT, **kw)


def dot_high(a, b, dims):
    return lax.dot_general(
        a, b, (dims, ((), ())), precision=lax.Precision.HIGHEST, preferred_element_type=F32
    )


def dot_bf16(a, b):
    return jnp.dot(a, b, preferred_element_type=F32)


def split(x):
    high = x.astype(BF16)
    low = (x - high.astype(F32)).astype(BF16)
    return high, low


def factor_pair(rows, cols, scale, count):
    inner = dot_high(rows, cols, ((1,), (1,)))
    row_sq = jnp.sum(rows * rows, axis=1, keepdims=True)
    ones = jnp.ones((8, rows.shape[1]), F32)
    col_sq = dot_high(ones, cols * cols, ((1,), (1,)))[0:1, :]
    dist = row_sq + col_sq - 2.0 * inner
    kern = jnp.exp(-dist / (2.0 * scale * scale)) * (1.0 / math.sqrt(count))
    deriv = kern * dist / (scale * scale * scale)
    return kern, deriv


def day_kernel(scales, embed, probe, residual, out, weights, rest):
    row = lax.broadcasted_iota(jnp.int32, (128, ND), 0)
    day = lax.broadcasted_iota(jnp.int32, (128, ND), 1)
    pick = (day == (row // 8) * 2 + row % 2).astype(F32)
    rows = dot_high(pick, embed[...], ((1,), (0,)))
    col = lax.broadcasted_iota(jnp.int32, (192, ND), 0)
    day = lax.broadcasted_iota(jnp.int32, (192, ND), 1)
    pick = (day == col % ND).astype(F32)
    cols = dot_high(pick, embed[...], ((1,), (0,)))
    kern, deriv = factor_pair(rows, cols, scales[2], ND)
    row = lax.broadcasted_iota(jnp.int32, (128, 192), 0)
    col = lax.broadcasted_iota(jnp.int32, (128, 192), 1)
    both = jnp.where((row // 2) % 2 == 1, deriv, kern)
    high = both.astype(BF16).astype(F32)
    part = jnp.where((col // ND) % 3 == 2, both - high, high)
    weights[...] = jnp.where((row // 4) % 2 == col // 96, part, 0.0).astype(BF16)
    rest[...] = jnp.zeros((2, ND, 128), F32)

    def operand(lat, at):
        rest[at, :, 0:REST] = probe[lat, :, 128:LOCAL_LON]
        rest[at, :, 64 : 64 + REST] = residual[lat, :, 128:LOCAL_LON]
        x = jnp.concatenate([probe[lat, :, 0:128], residual[lat, :, 0:128], rest[at]], axis=1)
        high, low = split(x)
        return [high, low, high]

    def store(pair, value):
        for dst in range(16):
            for block in range(3):
                out[dst, pl.ds(pair * 24 + block, 8, stride=3), :] = value[
                    dst * 8 : dst * 8 + 8, block * 128 : block * 128 + 128
                ]

    def step(pair, carry):
        stacked = jnp.concatenate(operand(2 * pair, 0) + operand(2 * pair + 1, 1), axis=0)
        store(pair, dot_bf16(weights[...], stacked))
        return carry

    lax.fori_loop(0, LATS // 2, step, 0)
    none = jnp.zeros((96, 384), BF16)
    stacked = jnp.concatenate(operand(LATS - 1, 0) + [none], axis=0)
    store(LATS // 2, dot_bf16(weights[...], stacked))


def day_products(scales, embed, probe, residual):
    return pl.pallas_call(
        day_kernel,
        out_shape=jax.ShapeDtypeStruct((16, DAY_ROWS, 128), F32),
        in_specs=[pl.BlockSpec(memory_space=pltpu.SMEM)]
        + [pl.BlockSpec(memory_space=pltpu.VMEM)] * 3,
        out_specs=pl.BlockSpec(memory_space=pltpu.VMEM),
        scratch_shapes=[pltpu.VMEM((128, 192), BF16), pltpu.VMEM((2, ND, 128), F32)],
        compiler_params=params(),
        name="day_products",
    )(scales, embed, probe, residual)


def factor_kernel(which, count, scales, rows, cols, high, low):
    kern, deriv = factor_pair(rows[...], cols[...], scales[which], count)
    for at, value in enumerate((kern, deriv)):
        high[at], low[at] = split(value)


def factor_halves(scales, which, count, rows, cols):
    nr, nc = rows.shape[0], cols.shape[0]
    shape = jax.ShapeDtypeStruct((2, nr, nc), BF16)
    block = pl.BlockSpec((2, 256, nc), lambda i: (0, i, 0))
    return pl.pallas_call(
        functools.partial(factor_kernel, which, count),
        grid=(nr // 256,),
        out_shape=(shape, shape),
        in_specs=[
            pl.BlockSpec(memory_space=pltpu.SMEM),
            pl.BlockSpec((256, 16), lambda i: (i, 0)),
            pl.BlockSpec((nc, 16), lambda i: (0, 0)),
        ],
        out_specs=(block, block),
        compiler_params=params(),
        cost_estimate=pl.CostEstimate(
            flops=2 * 96 * nr * nc, bytes_accessed=8 * nr * nc, transcendentals=nr * nc
        ),
        name="factors",
    )(scales, rows, cols)


def lat_kernel(op, moved, high, low, out):
    for block in range(3):
        parts = [
            split(moved[pl.ds((op * 2 + day) * 3 + block, 16 * SLOTS, stride=12), :])
            for day in range(2)
        ]
        x_high = jnp.concatenate([p[0] for p in parts], axis=1)
        x_low = jnp.concatenate([p[1] for p in parts], axis=1)
        value = dot_bf16(high[0], x_high) + dot_bf16(high[0], x_low) + dot_bf16(low[0], x_high)
        for dst in range(8):
            for day in range(2):
                out[dst, pl.ds(block * 180 + day, OUT_LATS, stride=2), :] = value[
                    dst * 96 : dst * 96 + OUT_LATS, day * 128 : day * 128 + 128
                ]


def lat_products(moved, high, low, op, which):
    factor = pl.BlockSpec((1, 768, 736), lambda i: (which, 0, 0))
    return pl.pallas_call(
        functools.partial(lat_kernel, op),
        grid=(1,),
        out_shape=jax.ShapeDtypeStruct((8, LAT_ROWS, 128), F32),
        in_specs=[pl.BlockSpec((16 * DAY_ROWS, 128), lambda i: (0, 0)), factor, factor],
        out_specs=pl.BlockSpec((8, LAT_ROWS, 128), lambda i: (0, 0, 0)),
        compiler_params=params(),
        cost_estimate=pl.CostEstimate(
            flops=2 * 3 * 768 * 768 * 768, bytes_accessed=10**7, transcendentals=0
        ),
        name="lat_products",
    )(moved, high, low)


def lon_kernel(moved, high, low, *rest):
    out, z_high, z_low = rest[-3:]

    @pl.when((pl.program_id(0) == 0) & (pl.program_id(1) == 0))
    def _():
        for src in range(8):
            at = pl.ds(src * 128, 128)
            z_high[:, at], z_low[:, at] = split(moved[src, 0:360, :])
        first = lax.broadcasted_iota(jnp.int32, (180, 128), 1) < 64
        for pair in range(4):
            one = moved[2 * pair, 360:540, :]
            two = moved[2 * pair + 1, 360:540, :]
            probe = jnp.where(first, one, pltpu.roll(two, 64, 1))
            residual = jnp.where(first, pltpu.roll(one, 64, 1), two)
            at = pl.ds(1024 + pair * 128, 128)
            z_high[:, at], z_low[:, at] = split(jnp.concatenate([probe, residual], axis=0))

    value = (
        dot_bf16(z_high[...], high[0])
        + dot_bf16(z_high[...], low[0])
        + dot_bf16(z_low[...], high[0])
    )
    out[:, 0] = value.reshape(2, OUT_LATS, 2, value.shape[1])


def lon_products(moved, high, low, operators, so_far=None):
    wide = 512
    factor = pl.BlockSpec((1, 1536, wide), lambda w, n: (w, 0, n))
    first, step = operators[0], operators[-1] - operators[0]
    in_specs = [pl.BlockSpec((8, LAT_ROWS, 128), lambda w, n: (0, 0, 0)), factor, factor]
    args = [moved, high, low]
    aliases = {}
    if so_far is not None:
        in_specs.append(pl.BlockSpec(memory_space=pl.ANY))
        args.append(so_far)
        aliases = {3: 0}
    return pl.pallas_call(
        lon_kernel,
        grid=(len(operators), pl.cdiv(NL, wide)),
        out_shape=jax.ShapeDtypeStruct((2, 4, OUT_LATS, 2, NL), F32),
        in_specs=in_specs,
        out_specs=pl.BlockSpec(
            (2, 1, OUT_LATS, 2, wide), lambda w, n: (0, first + step * w, 0, 0, n)
        ),
        scratch_shapes=[pltpu.VMEM((360, 1536), BF16)] * 2,
        input_output_aliases=aliases,
        compiler_params=params(),
        cost_estimate=pl.CostEstimate(
            flops=2 * 3 * 360 * 1536 * 1536 * len(operators),
            bytes_accessed=2 * 10**7,
            transcendentals=0,
        ),
        name="lon_products",
    )(*args)


def local(probe, residual, lon_embed, lat_embed, day_embed, scales):
    sent = day_products(
        scales, day_embed, jnp.transpose(probe, (1, 0, 2)), jnp.transpose(residual, (1, 0, 2))
    )
    moved = lax.all_to_all(sent, "lat", split_axis=0, concat_axis=0, tiled=True)
    moved = moved.reshape(16 * DAY_ROWS, 128)

    lat_rows = jnp.pad(lat_embed.reshape(8, 90, 16), ((0, 0), (0, 6), (0, 0))).reshape(768, 16)
    lat_cols = jnp.pad(lat_embed.reshape(16, 45, 16), ((0, 0), (0, 1), (0, 0))).reshape(736, 16)
    by_part = lon_embed.reshape(8, LOCAL_LON, 16)
    lon_rest = jnp.pad(by_part[:, 128:], ((0, 0), (0, 64 - REST), (0, 0)))
    lon_rows = jnp.concatenate(
        [by_part[:, :128].reshape(1024, 16), lon_rest.reshape(512, 16)], axis=0
    )
    lat_high, lat_low = factor_halves(scales, 1, NA, lat_rows, lat_cols)
    lon_high, lon_low = factor_halves(scales, 0, NL, lon_rows, lon_embed)

    result = None
    for op, which, operators in ((0, 0, (0, 2)), (1, 0, (1,)), (0, 1, (3,))):
        terms = lat_products(moved, lat_high, lat_low, op, which)
        terms = lax.all_to_all(terms, "lon", split_axis=0, concat_axis=0, tiled=True)
        result = lon_products(terms, lon_high, lon_low, operators, result)
    return jnp.transpose(result, (0, 1, 3, 2, 4))


def solution(mesh):
    placed = (P(None, "lat", "lon"), P(None, "lat", "lon"), P(), P(), P(), P())
    return jax.shard_map(
        local,
        mesh=mesh,
        in_specs=placed,
        out_specs=P(None, None, "lat", "lon", None),
        check_vma=False,
    )
```

```python
import functools
import math

import jax
import jax.numpy as jnp
from jax import lax
from jax.experimental import pallas as pl
from jax.experimental.pallas import tpu as pltpu
from jax.sharding import PartitionSpec as P

NL = 1440
NA = 720
ND = 32
F32 = jnp.float32
BF16 = jnp.bfloat16
VMEM_LIMIT = 58 * 1024 * 1024

LOCAL_LON = 180
REST = LOCAL_LON - 128
LATS = 45
SLOTS = 46
DAY_ROWS = SLOTS * 12
OUT_LATS = 90
KIND_ROWS = 2 * OUT_LATS


def params(**kw):
    return pltpu.CompilerParams(vmem_limit_bytes=VMEM_LIMIT, **kw)


def dot_high(a, b, dims):
    return lax.dot_general(
        a, b, (dims, ((), ())), precision=lax.Precision.HIGHEST, preferred_element_type=F32
    )


def dot_halves(a_high, a_low, b_high, b_low):
    def dot(a, b):
        return jnp.dot(a, b, preferred_element_type=F32)

    return dot(a_high, b_high) + dot(a_high, b_low) + dot(a_low, b_high)


def split(x):
    high = x.astype(BF16)
    low = (x - high.astype(F32)).astype(BF16)
    return high, low


def factor_pair(rows, cols, scale, count):
    inner = dot_high(rows, cols, ((1,), (1,)))
    row_sq = jnp.sum(rows * rows, axis=1, keepdims=True)
    ones = jnp.ones((8, rows.shape[1]), F32)
    col_sq = dot_high(ones, cols * cols, ((1,), (1,)))[0:1, :]
    dist = row_sq + col_sq - 2.0 * inner
    kern = jnp.exp(-dist / (2.0 * scale * scale)) * (1.0 / math.sqrt(count))
    deriv = kern * dist / (scale * scale * scale)
    return kern, deriv


PAIRS = 4


def day_kernel(scales, embed, probe, residual, out, weights):
    step = pl.program_id(0)

    @pl.when(step == 0)
    def _():
        row = lax.broadcasted_iota(jnp.int32, (128, ND), 0)
        day = lax.broadcasted_iota(jnp.int32, (128, ND), 1)
        pick = (day == (row // 8) * 2 + row % 2).astype(F32)
        rows = dot_high(pick, embed[...], ((1,), (1,)))
        col = lax.broadcasted_iota(jnp.int32, (192, ND), 0)
        day = lax.broadcasted_iota(jnp.int32, (192, ND), 1)
        pick = (day == col % ND).astype(F32)
        cols = dot_high(pick, embed[...], ((1,), (1,)))
        kern, deriv = factor_pair(rows, cols, scales[2], ND)
        row = lax.broadcasted_iota(jnp.int32, (128, 192), 0)
        col = lax.broadcasted_iota(jnp.int32, (128, 192), 1)
        both = jnp.where((row // 2) % 2 == 1, deriv, kern)
        high = both.astype(BF16).astype(F32)
        part = jnp.where((col // ND) % 3 == 2, both - high, high)
        weights[...] = jnp.where((row // 4) % 2 == col // 96, part, 0.0).astype(BF16)

    lane = lax.broadcasted_iota(jnp.int32, (ND, 128), 1)
    none = jnp.zeros((ND, 128 - REST), F32)

    def operand(lat):
        one = jnp.concatenate([probe[lat, :, 128:LOCAL_LON], none], axis=1)
        two = jnp.concatenate([residual[lat, :, 128:LOCAL_LON], none], axis=1)
        rest = jnp.where(lane < 64, one, pltpu.roll(two, 64, 1))
        x = jnp.concatenate([probe[lat, :, 0:128], residual[lat, :, 0:128], rest], axis=1)
        x = jnp.where(step * (2 * PAIRS) + lat < LATS, x, 0.0)
        high, low = split(x)
        return [high, low, high]

    for pair in range(PAIRS):
        stacked = jnp.concatenate(operand(2 * pair) + operand(2 * pair + 1), axis=0)
        value = jnp.dot(weights[...], stacked, preferred_element_type=F32)
        for dst in range(16):
            for block in range(3):
                out[dst, pl.ds(pair * 24 + block, 8, stride=3), :] = value[
                    dst * 8 : dst * 8 + 8, block * 128 : block * 128 + 128
                ]


def day_products(scales, embed, probe, residual):
    field = pl.BlockSpec((2 * PAIRS, ND, LOCAL_LON), lambda i: (i, 0, 0))
    return pl.pallas_call(
        day_kernel,
        grid=(pl.cdiv(SLOTS, 2 * PAIRS),),
        out_shape=jax.ShapeDtypeStruct((16, DAY_ROWS, 128), F32),
        in_specs=[
            pl.BlockSpec(memory_space=pltpu.SMEM),
            pl.BlockSpec((16, ND), lambda i: (0, 0)),
            field,
            field,
        ],
        out_specs=pl.BlockSpec((16, 24 * PAIRS, 128), lambda i: (0, i, 0)),
        scratch_shapes=[pltpu.VMEM((128, 192), BF16)],
        compiler_params=params(),
        name="day_products",
    )(scales, embed, probe, residual)


def factor_kernel(which, count, scales, rows, cols, high, low):
    kern, deriv = factor_pair(rows[...], cols[...], scales[which], count)
    for at, value in enumerate((kern, deriv)):
        high[at], low[at] = split(value)


def factor_halves(scales, which, count, rows, cols):
    nr, nc = rows.shape[0], cols.shape[0]
    shape = jax.ShapeDtypeStruct((2, nr, nc), BF16)
    block = pl.BlockSpec((2, 256, nc), lambda i: (0, i, 0))
    return pl.pallas_call(
        functools.partial(factor_kernel, which, count),
        grid=(nr // 256,),
        out_shape=(shape, shape),
        in_specs=[
            pl.BlockSpec(memory_space=pltpu.SMEM),
            pl.BlockSpec((256, 16), lambda i: (i, 0)),
            pl.BlockSpec((nc, 16), lambda i: (0, 0)),
        ],
        out_specs=(block, block),
        compiler_params=params(),
        cost_estimate=pl.CostEstimate(
            flops=2 * 96 * nr * nc, bytes_accessed=8 * nr * nc, transcendentals=nr * nc
        ),
        name="factors",
    )(scales, rows, cols)


TERM_ROWS = 544


def lat_kernel(kinds, moved, *refs):
    count = len(kinds)
    factors, outs = refs[: 2 * count], refs[2 * count : 10 * count]
    held, sems = refs[10 * count :]
    copies = []
    for at, (op, _) in enumerate(kinds):
        for block in range(3):
            parts = [
                split(moved[pl.ds((op * 2 + day) * 3 + block, 16 * SLOTS, stride=12), :])
                for day in range(2)
            ]
            x_high, x_low = [jnp.concatenate([p[half] for p in parts], axis=1) for half in range(2)]
            value = dot_halves(factors[2 * at][0], factors[2 * at + 1][0], x_high, x_low)
            for step in range(8):
                for day in range(2):
                    held[8 * at + step, pl.ds(block * KIND_ROWS + day, OUT_LATS, stride=2), :] = (
                        value[step * 96 : step * 96 + OUT_LATS, day * 128 : day * 128 + 128]
                    )
        for step in range(8):
            place = 8 * at + step
            copies.append(pltpu.make_async_copy(held.at[place], outs[place], sems.at[place]))
            copies[-1].start()
    for copy in copies:
        copy.wait()


def lat_products(moved, high, low, kinds):
    count = len(kinds)
    in_specs, args = [pl.BlockSpec((16 * DAY_ROWS, 128), lambda i: (0, 0))], [moved]
    for _, which in kinds:
        in_specs += [pl.BlockSpec((1, 768, 16 * SLOTS), lambda i, which=which: (which, 0, 0))] * 2
        args += [high, low]
    terms = pl.pallas_call(
        functools.partial(lat_kernel, kinds),
        grid=(1,),
        out_shape=[jax.ShapeDtypeStruct((TERM_ROWS, 128), F32)] * (8 * count),
        in_specs=in_specs,
        out_specs=[pl.BlockSpec(memory_space=pl.ANY)] * (8 * count),
        scratch_shapes=[
            pltpu.VMEM((8 * count, TERM_ROWS, 128), F32),
            pltpu.SemaphoreType.DMA((8 * count,)),
        ],
        compiler_params=params(),
        cost_estimate=pl.CostEstimate(
            flops=2 * 3 * 768 * 768 * 768 * count, bytes_accessed=10**7, transcendentals=0
        ),
        name="lat_products",
    )(*args)
    return [terms[8 * at : 8 * at + 8] for at in range(count)]


def lay_out(read, put, rows):
    for src in range(8):
        for field in range(2):
            put(field, src, read(src, field))
    first = lax.broadcasted_iota(jnp.int32, (rows, 128), 1) < 64
    for pair in range(4):
        one, two = read(2 * pair, 2), read(2 * pair + 1, 2)
        put(0, 8 + pair, jnp.where(first, one, pltpu.roll(two, 64, 1)))
        put(1, 8 + pair, jnp.where(first, pltpu.roll(one, 64, 1), two))


def by_day(value, start):
    return value[start : start + KIND_ROWS].reshape(OUT_LATS, 2, value.shape[1])


FIELD_ROWS = 192


def lon_kernel(count, *refs):
    terms, factors = refs[:8], refs[8 : 8 + 2 * count]
    out, z_high, z_low = refs[-3:]

    @pl.when(pl.program_id(0) == 0)
    def _():
        def read(step, block):
            return terms[step][block * KIND_ROWS : block * KIND_ROWS + KIND_ROWS, :]

        def put(field, col, value):
            at = pl.ds(col * 128, 128)
            for z, half in zip((z_high, z_low), split(value)):
                z[field * FIELD_ROWS : field * FIELD_ROWS + KIND_ROWS, at] = half

        lay_out(read, put, KIND_ROWS)

    for at in range(count):
        high, low = factors[2 * at : 2 * at + 2]
        value = dot_halves(z_high[...], z_low[...], high[0], low[0])
        for field in range(2):
            out[field, at, 0] = by_day(value, field * FIELD_ROWS)


def lon_products(terms, high, low, operators, so_far=None, wide=512):
    count = len(operators)
    high_at, low_at = divmod(operators[0], 2)
    in_specs = [pl.BlockSpec((TERM_ROWS, 128), lambda n: (0, 0))] * 8
    args = list(terms)
    for which in range(count):
        in_specs += [pl.BlockSpec((1, 1536, wide), lambda n, which=which: (which, 0, n))] * 2
        args += [high, low]
    aliases = {}
    if so_far is not None:
        aliases = {len(args): 0}
        in_specs.append(pl.BlockSpec(memory_space=pl.ANY))
        args.append(so_far)
    return pl.pallas_call(
        functools.partial(lon_kernel, count),
        grid=(pl.cdiv(NL, wide),),
        out_shape=jax.ShapeDtypeStruct((2, 2, 2, OUT_LATS, 2, NL), F32),
        in_specs=in_specs,
        out_specs=pl.BlockSpec(
            (2, count, 1, OUT_LATS, 2, wide), lambda n: (0, high_at, low_at, 0, 0, n)
        ),
        scratch_shapes=[pltpu.VMEM((2 * FIELD_ROWS, 1536), BF16)] * 2,
        input_output_aliases=aliases,
        compiler_params=params(),
        cost_estimate=pl.CostEstimate(
            flops=2 * 3 * 360 * 1536 * 1536 * count, bytes_accessed=2 * 10**7, transcendentals=0
        ),
        name="lon_products",
    )(*args)


ORDER = (1, 6, 4, 3, 2, 5, 7)


def local(probe, residual, lon_embed, lat_embed, day_embed, scales):
    sent = day_products(
        scales, day_embed.T, jnp.transpose(probe, (1, 0, 2)), jnp.transpose(residual, (1, 0, 2))
    )
    moved = lax.all_to_all(sent, "lat", split_axis=0, concat_axis=0, tiled=True)
    moved = moved.reshape(16 * DAY_ROWS, 128)

    order = jnp.bitwise_xor(lax.axis_index("lon"), jnp.arange(8))
    by_block = lat_embed.reshape(8, OUT_LATS, 16)[order]
    lat_rows = jnp.pad(by_block, ((0, 0), (0, 6), (0, 0))).reshape(768, 16)
    lat_cols = jnp.pad(lat_embed.reshape(16, LATS, 16), ((0, 0), (0, SLOTS - LATS), (0, 0)))
    by_block = lon_embed.reshape(8, LOCAL_LON, 16)[order]
    lon_rest = jnp.pad(by_block[:, 128:], ((0, 0), (0, 64 - REST), (0, 0)))
    lon_rows = jnp.concatenate(
        [by_block[:, :128].reshape(1024, 16), lon_rest.reshape(512, 16)], axis=0
    )
    lat_factors = factor_halves(scales, 1, NA, lat_rows, lat_cols.reshape(16 * SLOTS, 16))
    lon_factors = factor_halves(scales, 0, NL, lon_rows, lon_embed)
    moved, lat_factors, lon_factors = lax.optimization_barrier((moved, lat_factors, lon_factors))

    def exchanged(terms):
        there = {0: terms[0]}
        for step in ORDER:
            pairs = [(i, i ^ step) for i in range(8)]
            there[step] = lax.ppermute(terms[step], "lon", pairs)
        return [there[step] for step in range(8)]

    (plain,) = lat_products(moved, *lat_factors, ((0, 0),))
    by_day, by_lat = lat_products(moved, *lat_factors, ((1, 0), (0, 1)))
    result = lon_products(exchanged(plain), *lon_factors, (0, 2))
    result = lon_products(exchanged(by_day), *lon_factors, (1,), result)
    result = lon_products(exchanged(by_lat), *lon_factors, (3,), result)
    result = result.reshape(2, 4, OUT_LATS, 2, NL)
    return jnp.transpose(result, (0, 1, 3, 2, 4))


def solution(mesh):
    placed = (P(None, "lat", "lon"), P(None, "lat", "lon"), P(), P(), P(), P())
    return jax.shard_map(
        local,
        mesh=mesh,
        in_specs=placed,
        out_specs=P(None, None, "lat", "lon", None),
        check_vma=False,
    )
```

```python
import functools
import math

import jax
import jax.numpy as jnp
from jax import lax
from jax.experimental import pallas as pl
from jax.experimental.pallas import tpu as pltpu
from jax.sharding import PartitionSpec as P

NL = 1440
NA = 720
ND = 32
F32 = jnp.float32
BF16 = jnp.bfloat16
VMEM_LIMIT = 58 * 1024 * 1024

LOCAL_LON = 180
REST = LOCAL_LON - 128
LATS = 45
SLOTS = 46
DAY_ROWS = SLOTS * 12
OUT_LATS = 90
KIND_ROWS = 2 * OUT_LATS


def params(mib=58):
    return pltpu.CompilerParams(vmem_limit_bytes=mib * 1024 * 1024)


def dot_high(a, b, dims):
    return lax.dot_general(
        a, b, (dims, ((), ())), precision=lax.Precision.HIGHEST, preferred_element_type=F32
    )


def dot_halves(a_high, a_low, b_high, b_low):
    def dot(a, b):
        return jnp.dot(a, b, preferred_element_type=F32)

    return dot(a_high, b_high) + dot(a_high, b_low) + dot(a_low, b_high)


def split(x):
    high = x.astype(BF16)
    low = (x - high.astype(F32)).astype(BF16)
    return high, low


def factor_pair(rows, cols, scale, count):
    inner = dot_high(rows, cols, ((1,), (1,)))
    row_sq = jnp.sum(rows * rows, axis=1, keepdims=True)
    ones = jnp.ones((8, rows.shape[1]), F32)
    col_sq = dot_high(ones, cols * cols, ((1,), (1,)))[0:1, :]
    dist = row_sq + col_sq - 2.0 * inner
    kern = jnp.exp(-dist / (2.0 * scale * scale)) * (1.0 / math.sqrt(count))
    deriv = kern * dist / (scale * scale * scale)
    return kern, deriv


PAIRS = 4


def day_kernel(scales, embed, probe, residual, out, weights):
    step = pl.program_id(0)

    @pl.when(step == 0)
    def _():
        row = lax.broadcasted_iota(jnp.int32, (128, ND), 0)
        day = lax.broadcasted_iota(jnp.int32, (128, ND), 1)
        pick = (day == (row // 8) * 2 + row % 2).astype(F32)
        rows = dot_high(pick, embed[...], ((1,), (1,)))
        col = lax.broadcasted_iota(jnp.int32, (192, ND), 0)
        day = lax.broadcasted_iota(jnp.int32, (192, ND), 1)
        pick = (day == col % ND).astype(F32)
        cols = dot_high(pick, embed[...], ((1,), (1,)))
        kern, deriv = factor_pair(rows, cols, scales[2], ND)
        row = lax.broadcasted_iota(jnp.int32, (128, 192), 0)
        col = lax.broadcasted_iota(jnp.int32, (128, 192), 1)
        both = jnp.where((row // 2) % 2 == 1, deriv, kern)
        high = both.astype(BF16).astype(F32)
        part = jnp.where((col // ND) % 3 == 2, both - high, high)
        weights[...] = jnp.where((row // 4) % 2 == col // 96, part, 0.0).astype(BF16)

    lane = lax.broadcasted_iota(jnp.int32, (ND, 128), 1)
    none = jnp.zeros((ND, 128 - REST), F32)

    def operand(lat):
        one = jnp.concatenate([probe[lat, :, 128:LOCAL_LON], none], axis=1)
        two = jnp.concatenate([residual[lat, :, 128:LOCAL_LON], none], axis=1)
        rest = jnp.where(lane < 64, one, pltpu.roll(two, 64, 1))
        x = jnp.concatenate([probe[lat, :, 0:128], residual[lat, :, 0:128], rest], axis=1)
        x = jnp.where(step * (2 * PAIRS) + lat < LATS, x, 0.0)
        high, low = split(x)
        return [high, low, high]

    for pair in range(PAIRS):
        stacked = jnp.concatenate(operand(2 * pair) + operand(2 * pair + 1), axis=0)
        value = jnp.dot(weights[...], stacked, preferred_element_type=F32)
        for dst in range(16):
            for block in range(3):
                out[dst, pl.ds(pair * 24 + block, 8, stride=3), :] = value[
                    dst * 8 : dst * 8 + 8, block * 128 : block * 128 + 128
                ]


def day_products(scales, embed, probe, residual):
    field = pl.BlockSpec((2 * PAIRS, ND, LOCAL_LON), lambda i: (i, 0, 0))
    return pl.pallas_call(
        day_kernel,
        grid=(pl.cdiv(SLOTS, 2 * PAIRS),),
        out_shape=jax.ShapeDtypeStruct((16, DAY_ROWS, 128), F32),
        in_specs=[
            pl.BlockSpec(memory_space=pltpu.SMEM),
            pl.BlockSpec((16, ND), lambda i: (0, 0)),
            field,
            field,
        ],
        out_specs=pl.BlockSpec((16, 24 * PAIRS, 128), lambda i: (0, i, 0)),
        scratch_shapes=[pltpu.VMEM((128, 192), BF16)],
        compiler_params=params(),
        name="day_products",
    )(scales, embed, probe, residual)


def factor_kernel(which, count, scales, rows, cols, high, low):
    kern, deriv = factor_pair(rows[...], cols[...], scales[which], count)
    for at, value in enumerate((kern, deriv)):
        high[at], low[at] = split(value)


def factor_halves(scales, which, count, rows, cols, held=False):
    nr, nc = rows.shape[0], cols.shape[0]
    shape = (pltpu.VMEM if held else jax.ShapeDtypeStruct)((2, nr, nc), BF16)
    block = pl.BlockSpec((2, 256, nc), lambda i: (0, i, 0))
    return pl.pallas_call(
        functools.partial(factor_kernel, which, count),
        grid=(nr // 256,),
        out_shape=(shape, shape),
        in_specs=[
            pl.BlockSpec(memory_space=pltpu.SMEM),
            pl.BlockSpec((256, 16), lambda i: (i, 0)),
            pl.BlockSpec((nc, 16), lambda i: (0, 0)),
        ],
        out_specs=(block, block),
        compiler_params=params(30),
        cost_estimate=pl.CostEstimate(
            flops=2 * 96 * nr * nc, bytes_accessed=8 * nr * nc, transcendentals=nr * nc
        ),
        name="factors",
    )(scales, rows, cols)


TERM_ROWS = 544


def lat_kernel(kinds, moved, *refs):
    count = len(kinds)
    factors, outs = refs[: 2 * count], refs[2 * count : 10 * count]
    held, sems = refs[10 * count :]
    copies = []
    for at, (op, _) in enumerate(kinds):
        for block in range(3):
            parts = [
                split(moved[pl.ds((op * 2 + day) * 3 + block, 16 * SLOTS, stride=12), :])
                for day in range(2)
            ]
            x_high, x_low = [jnp.concatenate([p[half] for p in parts], axis=1) for half in range(2)]
            value = dot_halves(factors[2 * at][0], factors[2 * at + 1][0], x_high, x_low)
            for step in range(8):
                for day in range(2):
                    held[8 * at + step, pl.ds(block * KIND_ROWS + day, OUT_LATS, stride=2), :] = (
                        value[step * 96 : step * 96 + OUT_LATS, day * 128 : day * 128 + 128]
                    )
        for step in range(8):
            place = 8 * at + step
            copies.append(pltpu.make_async_copy(held.at[place], outs[place], sems.at[place]))
            copies[-1].start()
    for copy in copies:
        copy.wait()


def lat_products(moved, high, low, kinds):
    count = len(kinds)
    in_specs, args = [pl.BlockSpec((16 * DAY_ROWS, 128), lambda i: (0, 0))], [moved]
    for _, which in kinds:
        in_specs += [pl.BlockSpec((1, 768, 16 * SLOTS), lambda i, which=which: (which, 0, 0))] * 2
        args += [pltpu.with_memory_space_constraint(x, pltpu.HBM) for x in (high, low)]
    terms = pl.pallas_call(
        functools.partial(lat_kernel, kinds),
        grid=(1,),
        out_shape=[jax.ShapeDtypeStruct((TERM_ROWS, 128), F32)] * (8 * count),
        in_specs=in_specs,
        out_specs=[pl.BlockSpec(memory_space=pl.ANY)] * (8 * count),
        scratch_shapes=[
            pltpu.VMEM((8 * count, TERM_ROWS, 128), F32),
            pltpu.SemaphoreType.DMA((8 * count,)),
        ],
        compiler_params=params(28),
        cost_estimate=pl.CostEstimate(
            flops=2 * 3 * 768 * 768 * 768 * count, bytes_accessed=10**7, transcendentals=0
        ),
        name="lat_products",
    )(*args)
    return [terms[8 * at : 8 * at + 8] for at in range(count)]


def lay_out(read, put, rows):
    for src in range(8):
        for field in range(2):
            put(field, src, read(src, field))
    first = lax.broadcasted_iota(jnp.int32, (rows, 128), 1) < 64
    for pair in range(4):
        one, two = read(2 * pair, 2), read(2 * pair + 1, 2)
        put(0, 8 + pair, jnp.where(first, one, pltpu.roll(two, 64, 1)))
        put(1, 8 + pair, jnp.where(first, pltpu.roll(one, 64, 1), two))


def by_day(value, start):
    return value[start : start + KIND_ROWS].reshape(OUT_LATS, 2, value.shape[1])


WIDE = 1536
FIELD_ROWS = 192


def lon_kernel(count, *refs):
    terms, (high, low) = refs[:8], refs[8:10]
    out, z_high, z_low = refs[-3:]
    wide = out.shape[-1]
    cols = pl.ds(pl.multiple_of(pl.program_id(0) * wide, wide), wide)

    @pl.when(pl.program_id(0) == 0)
    def _():
        def read(step, block):
            return terms[step][block * KIND_ROWS : block * KIND_ROWS + KIND_ROWS, :]

        def put(field, col, value):
            at = pl.ds(col * 128, 128)
            for z, half in zip((z_high, z_low), split(value)):
                z[field * FIELD_ROWS : field * FIELD_ROWS + KIND_ROWS, at] = half

        lay_out(read, put, KIND_ROWS)

    for at in range(count):
        value = dot_halves(z_high[...], z_low[...], high[at, :, cols], low[at, :, cols])
        for field in range(2):
            out[field, at, 0] = by_day(value, field * FIELD_ROWS)


def lon_products(terms, high, low, operators, so_far=None, wide=512):
    count = len(operators)
    high_at, low_at = divmod(operators[0], 2)
    in_specs = [pl.BlockSpec((TERM_ROWS, 128), lambda n: (0, 0))] * 8
    in_specs += [pl.BlockSpec(memory_space=pltpu.VMEM)] * 2
    args = [*terms] + [pltpu.with_memory_space_constraint(x, pltpu.VMEM) for x in (high, low)]
    aliases = {}
    if so_far is not None:
        aliases = {len(args): 0}
        in_specs.append(pl.BlockSpec(memory_space=pl.ANY))
        args.append(so_far)
    return pl.pallas_call(
        functools.partial(lon_kernel, count),
        grid=(pl.cdiv(NL, wide),),
        out_shape=jax.ShapeDtypeStruct((2, 2, 2, OUT_LATS, 2, NL), F32),
        in_specs=in_specs,
        out_specs=pl.BlockSpec(
            (2, count, 1, OUT_LATS, 2, wide), lambda n: (0, high_at, low_at, 0, 0, n)
        ),
        scratch_shapes=[pltpu.VMEM((2 * FIELD_ROWS, 1536), BF16)] * 2,
        input_output_aliases=aliases,
        compiler_params=params(18),
        cost_estimate=pl.CostEstimate(
            flops=2 * 3 * 360 * 1536 * 1536 * count, bytes_accessed=2 * 10**7, transcendentals=0
        ),
        name="lon_products",
    )(*args)


STEPS = (0, 1, 6, 4, 3, 2, 5, 7)


def local(probe, residual, lon_embed, lat_embed, day_embed, scales):
    sent = day_products(
        scales, day_embed.T, jnp.transpose(probe, (1, 0, 2)), jnp.transpose(residual, (1, 0, 2))
    )
    moved = lax.all_to_all(sent, "lat", split_axis=0, concat_axis=0, tiled=True)
    moved = moved.reshape(16 * DAY_ROWS, 128)

    order = jnp.bitwise_xor(lax.axis_index("lon"), jnp.array(STEPS))
    by_block = lat_embed.reshape(8, OUT_LATS, 16)[order]
    lat_rows = jnp.pad(by_block, ((0, 0), (0, 6), (0, 0))).reshape(768, 16)
    lat_cols = jnp.pad(lat_embed.reshape(16, LATS, 16), ((0, 0), (0, SLOTS - LATS), (0, 0)))
    by_block = lon_embed.reshape(8, LOCAL_LON, 16)[order]
    lon_rest = jnp.pad(by_block[:, 128:], ((0, 0), (0, 64 - REST), (0, 0)))
    lon_rows = jnp.concatenate(
        [by_block[:, :128].reshape(1024, 16), lon_rest.reshape(512, 16)], axis=0
    )
    lat_factors = factor_halves(scales, 1, NA, lat_rows, lat_cols.reshape(16 * SLOTS, 16))
    lon_cols = jnp.pad(lon_embed, ((0, WIDE - NL), (0, 0)))
    lon_factors = factor_halves(scales, 0, NL, lon_rows, lon_cols, held=True)
    moved, lat_factors, lon_factors = lax.optimization_barrier((moved, lat_factors, lon_factors))

    def exchanged(terms):
        return [terms[0]] + [
            lax.ppermute(term, "lon", [(i, i ^ step) for i in range(8)])
            for term, step in zip(terms[1:], STEPS[1:])
        ]

    (plain,) = lat_products(moved, *lat_factors, ((0, 0),))
    by_day, by_lat = lat_products(moved, *lat_factors, ((1, 0), (0, 1)))
    result = lon_products(exchanged(plain), *lon_factors, (0, 2))
    result = lon_products(exchanged(by_day), *lon_factors, (1,), result)
    result = lon_products(exchanged(by_lat), *lon_factors, (3,), result)
    result = result.reshape(2, 4, OUT_LATS, 2, NL)
    return jnp.transpose(result, (0, 1, 3, 2, 4))


def solution(mesh):
    placed = (P(None, "lat", "lon"), P(None, "lat", "lon"), P(), P(), P(), P())
    return jax.shard_map(
        local,
        mesh=mesh,
        in_specs=placed,
        out_specs=P(None, None, "lat", "lon", None),
        check_vma=False,
    )
```

```python
import functools
import math

import jax
import jax.numpy as jnp
from jax import lax
from jax.experimental import pallas as pl
from jax.experimental.pallas import tpu as pltpu
from jax.sharding import PartitionSpec as P

NL = 1440
NA = 720
ND = 32
F32 = jnp.float32
BF16 = jnp.bfloat16
VMEM_LIMIT = 58 * 1024 * 1024

LOCAL_LON = 180
REST = LOCAL_LON - 128
LATS = 45
SLOTS = 46
DAY_ROWS = SLOTS * 12
OUT_LATS = 90
KIND_ROWS = 2 * OUT_LATS


def params(mib=58):
    return pltpu.CompilerParams(vmem_limit_bytes=mib * 1024 * 1024)


def dot_high(a, b, dims):
    return lax.dot_general(
        a, b, (dims, ((), ())), precision=lax.Precision.HIGHEST, preferred_element_type=F32
    )


def dot_halves(a_high, a_low, b_high, b_low):
    def dot(a, b):
        return jnp.dot(a, b, preferred_element_type=F32)

    return dot(a_high, b_high) + dot(a_high, b_low) + dot(a_low, b_high)


def split(x):
    high = x.astype(BF16)
    low = (x - high.astype(F32)).astype(BF16)
    return high, low


def factor_pair(rows, cols, scale, count):
    inner = dot_high(rows, cols, ((1,), (1,)))
    row_sq = jnp.sum(rows * rows, axis=1, keepdims=True)
    ones = jnp.ones((8, rows.shape[1]), F32)
    col_sq = dot_high(ones, cols * cols, ((1,), (1,)))[0:1, :]
    dist = row_sq + col_sq - 2.0 * inner
    kern = jnp.exp(-dist / (2.0 * scale * scale)) * (1.0 / math.sqrt(count))
    deriv = kern * dist / (scale * scale * scale)
    return kern, deriv


PAIRS = 12


def day_kernel(scales, embed, probe, residual, out, weights):
    step = pl.program_id(0)

    @pl.when(step == 0)
    def _():
        row = lax.broadcasted_iota(jnp.int32, (128, ND), 0)
        day = lax.broadcasted_iota(jnp.int32, (128, ND), 1)
        pick = (day == (row // 8) * 2 + row % 2).astype(F32)
        rows = dot_high(pick, embed[...], ((1,), (1,)))
        col = lax.broadcasted_iota(jnp.int32, (192, ND), 0)
        day = lax.broadcasted_iota(jnp.int32, (192, ND), 1)
        pick = (day == col % ND).astype(F32)
        cols = dot_high(pick, embed[...], ((1,), (1,)))
        kern, deriv = factor_pair(rows, cols, scales[2], ND)
        row = lax.broadcasted_iota(jnp.int32, (128, 192), 0)
        col = lax.broadcasted_iota(jnp.int32, (128, 192), 1)
        both = jnp.where((row // 2) % 2 == 1, deriv, kern)
        high = both.astype(BF16).astype(F32)
        part = jnp.where((col // ND) % 3 == 2, both - high, high)
        weights[...] = jnp.where((row // 4) % 2 == col // 96, part, 0.0).astype(BF16)

    lane = lax.broadcasted_iota(jnp.int32, (ND, 128), 1)
    none = jnp.zeros((ND, 128 - REST), F32)

    def operand(lat):
        one = jnp.concatenate([probe[lat, :, 128:LOCAL_LON], none], axis=1)
        two = jnp.concatenate([residual[lat, :, 128:LOCAL_LON], none], axis=1)
        rest = jnp.where(lane < 64, one, pltpu.roll(two, 64, 1))
        x = jnp.concatenate([probe[lat, :, 0:128], residual[lat, :, 0:128], rest], axis=1)
        x = jnp.where(step * (2 * PAIRS) + lat < LATS, x, 0.0)
        high, low = split(x)
        return [high, low, high]

    for pair in range(PAIRS):
        stacked = jnp.concatenate(operand(2 * pair) + operand(2 * pair + 1), axis=0)
        value = jnp.dot(weights[...], stacked, preferred_element_type=F32)
        for dst in range(16):
            for block in range(3):
                out[dst, pl.ds(pair * 24 + block, 8, stride=3), :] = value[
                    dst * 8 : dst * 8 + 8, block * 128 : block * 128 + 128
                ]


def day_products(scales, embed, probe, residual):
    field = pl.BlockSpec((2 * PAIRS, ND, LOCAL_LON), lambda i: (i, 0, 0))
    return pl.pallas_call(
        day_kernel,
        grid=(pl.cdiv(SLOTS, 2 * PAIRS),),
        out_shape=jax.ShapeDtypeStruct((16, DAY_ROWS, 128), F32),
        in_specs=[
            pl.BlockSpec(memory_space=pltpu.SMEM),
            pl.BlockSpec((16, ND), lambda i: (0, 0)),
            field,
            field,
        ],
        out_specs=pl.BlockSpec((16, 24 * PAIRS, 128), lambda i: (0, i, 0)),
        scratch_shapes=[pltpu.VMEM((128, 192), BF16)],
        compiler_params=params(),
        name="day_products",
    )(scales, embed, probe, residual)


def factor_kernel(which, count, scales, rows, cols, high, low):
    kern, deriv = factor_pair(rows[...], cols[...], scales[which], count)
    for at, value in enumerate((kern, deriv)):
        high[at], low[at] = split(value)


def factor_halves(scales, which, count, rows, cols, held=False):
    nr, nc = rows.shape[0], cols.shape[0]
    shape = (pltpu.VMEM if held else jax.ShapeDtypeStruct)((2, nr, nc), BF16)
    block = pl.BlockSpec((2, 256, nc), lambda i: (0, i, 0))
    return pl.pallas_call(
        functools.partial(factor_kernel, which, count),
        grid=(nr // 256,),
        out_shape=(shape, shape),
        in_specs=[
            pl.BlockSpec(memory_space=pltpu.SMEM),
            pl.BlockSpec((256, 16), lambda i: (i, 0)),
            pl.BlockSpec((nc, 16), lambda i: (0, 0)),
        ],
        out_specs=(block, block),
        compiler_params=params(30),
        cost_estimate=pl.CostEstimate(
            flops=2 * 96 * nr * nc, bytes_accessed=8 * nr * nc, transcendentals=nr * nc
        ),
        name="factors",
    )(scales, rows, cols)


TERM_ROWS = 544


def lat_kernel(kinds, moved, *refs):
    count = len(kinds)
    factors, outs = refs[: 2 * count], refs[2 * count : 10 * count]
    held, sems = refs[10 * count :]
    copies = []
    for at, (op, _) in enumerate(kinds):
        for block in range(3):
            parts = [
                split(moved[pl.ds((op * 2 + day) * 3 + block, 16 * SLOTS, stride=12), :])
                for day in range(2)
            ]
            x_high, x_low = [jnp.concatenate([p[half] for p in parts], axis=1) for half in range(2)]
            value = dot_halves(factors[2 * at][0], factors[2 * at + 1][0], x_high, x_low)
            for step in range(8):
                for day in range(2):
                    held[8 * at + step, pl.ds(block * KIND_ROWS + day, OUT_LATS, stride=2), :] = (
                        value[step * 96 : step * 96 + OUT_LATS, day * 128 : day * 128 + 128]
                    )
        for step in range(8):
            place = 8 * at + step
            copies.append(pltpu.make_async_copy(held.at[place], outs[place], sems.at[place]))
            copies[-1].start()
    for copy in copies:
        copy.wait()


def lat_products(moved, high, low, kinds):
    count = len(kinds)
    in_specs, args = [pl.BlockSpec((16 * DAY_ROWS, 128), lambda i: (0, 0))], [moved]
    for _, which in kinds:
        in_specs += [pl.BlockSpec((1, 768, 16 * SLOTS), lambda i, which=which: (which, 0, 0))] * 2
        args += [pltpu.with_memory_space_constraint(x, pltpu.HBM) for x in (high, low)]
    terms = pl.pallas_call(
        functools.partial(lat_kernel, kinds),
        grid=(1,),
        out_shape=[jax.ShapeDtypeStruct((TERM_ROWS, 128), F32)] * (8 * count),
        in_specs=in_specs,
        out_specs=[pl.BlockSpec(memory_space=pl.ANY)] * (8 * count),
        scratch_shapes=[
            pltpu.VMEM((8 * count, TERM_ROWS, 128), F32),
            pltpu.SemaphoreType.DMA((8 * count,)),
        ],
        compiler_params=params(28),
        cost_estimate=pl.CostEstimate(
            flops=2 * 3 * 768 * 768 * 768 * count, bytes_accessed=10**7, transcendentals=0
        ),
        name="lat_products",
    )(*args)
    return [terms[8 * at : 8 * at + 8] for at in range(count)]


def lay_out(read, put, rows):
    for src in range(8):
        for field in range(2):
            put(field, src, read(src, field))
    first = lax.broadcasted_iota(jnp.int32, (rows, 128), 1) < 64
    for pair in range(4):
        one, two = read(2 * pair, 2), read(2 * pair + 1, 2)
        put(0, 8 + pair, jnp.where(first, one, pltpu.roll(two, 64, 1)))
        put(1, 8 + pair, jnp.where(first, pltpu.roll(one, 64, 1), two))


def by_day(value, start):
    return value[start : start + KIND_ROWS].reshape(OUT_LATS, 2, value.shape[1])


WIDE = 1536
FIELD_ROWS = 192


def lon_kernel(count, *refs):
    terms, (high, low) = refs[:8], refs[8:10]
    out, z_high, z_low = refs[-3:]
    wide = out.shape[-1]
    cols = pl.ds(pl.multiple_of(pl.program_id(0) * wide, wide), wide)

    @pl.when(pl.program_id(0) == 0)
    def _():
        def read(step, block):
            return terms[step][block * KIND_ROWS : block * KIND_ROWS + KIND_ROWS, :]

        def put(field, col, value):
            at = pl.ds(col * 128, 128)
            for z, half in zip((z_high, z_low), split(value)):
                z[field * FIELD_ROWS : field * FIELD_ROWS + KIND_ROWS, at] = half

        lay_out(read, put, KIND_ROWS)

    for at in range(count):
        value = dot_halves(z_high[...], z_low[...], high[at, :, cols], low[at, :, cols])
        for field in range(2):
            out[field, at, 0] = by_day(value, field * FIELD_ROWS)


def lon_products(terms, high, low, operators, so_far=None, wide=512):
    count = len(operators)
    high_at, low_at = divmod(operators[0], 2)
    in_specs = [pl.BlockSpec((TERM_ROWS, 128), lambda n: (0, 0))] * 8
    in_specs += [pl.BlockSpec(memory_space=pltpu.VMEM)] * 2
    args = [*terms] + [pltpu.with_memory_space_constraint(x, pltpu.VMEM) for x in (high, low)]
    aliases = {}
    if so_far is not None:
        aliases = {len(args): 0}
        in_specs.append(pl.BlockSpec(memory_space=pl.ANY))
        args.append(so_far)
    return pl.pallas_call(
        functools.partial(lon_kernel, count),
        grid=(pl.cdiv(NL, wide),),
        out_shape=jax.ShapeDtypeStruct((2, 2, 2, OUT_LATS, 2, NL), F32),
        in_specs=in_specs,
        out_specs=pl.BlockSpec(
            (2, count, 1, OUT_LATS, 2, wide), lambda n: (0, high_at, low_at, 0, 0, n)
        ),
        scratch_shapes=[pltpu.VMEM((2 * FIELD_ROWS, 1536), BF16)] * 2,
        input_output_aliases=aliases,
        compiler_params=params(18),
        cost_estimate=pl.CostEstimate(
            flops=2 * 3 * 360 * 1536 * 1536 * count, bytes_accessed=2 * 10**7, transcendentals=0
        ),
        name="lon_products",
    )(*args)


STEPS = (0, 1, 6, 4, 3, 2, 5, 7)


def local(probe, residual, lon_embed, lat_embed, day_embed, scales):
    sent = day_products(
        scales, day_embed.T, jnp.transpose(probe, (1, 0, 2)), jnp.transpose(residual, (1, 0, 2))
    )
    moved = lax.all_to_all(sent, "lat", split_axis=0, concat_axis=0, tiled=True)
    moved = moved.reshape(16 * DAY_ROWS, 128)

    order = jnp.bitwise_xor(lax.axis_index("lon"), jnp.array(STEPS))
    by_block = lat_embed.reshape(8, OUT_LATS, 16)[order]
    lat_rows = jnp.pad(by_block, ((0, 0), (0, 6), (0, 0))).reshape(768, 16)
    lat_cols = jnp.pad(lat_embed.reshape(16, LATS, 16), ((0, 0), (0, SLOTS - LATS), (0, 0)))
    by_block = lon_embed.reshape(8, LOCAL_LON, 16)[order]
    lon_rest = jnp.pad(by_block[:, 128:], ((0, 0), (0, 64 - REST), (0, 0)))
    lon_rows = jnp.concatenate(
        [by_block[:, :128].reshape(1024, 16), lon_rest.reshape(512, 16)], axis=0
    )
    lat_factors = factor_halves(scales, 1, NA, lat_rows, lat_cols.reshape(16 * SLOTS, 16))
    lon_cols = jnp.pad(lon_embed, ((0, WIDE - NL), (0, 0)))
    lon_factors = factor_halves(scales, 0, NL, lon_rows, lon_cols, held=True)
    moved, lat_factors, lon_factors = lax.optimization_barrier((moved, lat_factors, lon_factors))

    def exchanged(terms):
        return [terms[0]] + [
            lax.ppermute(term, "lon", [(i, i ^ step) for i in range(8)])
            for term, step in zip(terms[1:], STEPS[1:])
        ]

    (plain,) = lat_products(moved, *lat_factors, ((0, 0),))
    (by_day,) = lat_products(moved, *lat_factors, ((1, 0),))
    (by_lat,) = lat_products(moved, *lat_factors, ((0, 1),))
    result = lon_products(exchanged(plain), *lon_factors, (0, 2))
    result = lon_products(exchanged(by_day), *lon_factors, (1,), result)
    result = lon_products(exchanged(by_lat), *lon_factors, (3,), result)
    result = result.reshape(2, 4, OUT_LATS, 2, NL)
    return jnp.transpose(result, (0, 1, 3, 2, 4))


def solution(mesh):
    placed = (P(None, "lat", "lon"), P(None, "lat", "lon"), P(), P(), P(), P())
    return jax.shard_map(
        local,
        mesh=mesh,
        in_specs=placed,
        out_specs=P(None, None, "lat", "lon", None),
        check_vma=False,
    )
```

```python
import functools
import math

import jax
import jax.numpy as jnp
from jax import lax
from jax.experimental import pallas as pl
from jax.experimental.pallas import tpu as pltpu
from jax.sharding import PartitionSpec as P

NL = 1440
NA = 720
ND = 32
F32 = jnp.float32
BF16 = jnp.bfloat16
VMEM_LIMIT = 58 * 1024 * 1024

LOCAL_LON = 180
REST = LOCAL_LON - 128
LATS = 45
SLOTS = 46
DAY_ROWS = SLOTS * 12
OUT_LATS = 90
KIND_ROWS = 2 * OUT_LATS


def params(mib=58):
    return pltpu.CompilerParams(vmem_limit_bytes=mib * 1024 * 1024)


def dot_high(a, b, dims):
    return lax.dot_general(
        a, b, (dims, ((), ())), precision=lax.Precision.HIGHEST, preferred_element_type=F32
    )


def dot_halves(a_high, a_low, b_high, b_low):
    def dot(a, b):
        return jnp.dot(a, b, preferred_element_type=F32)

    return dot(a_high, b_high) + dot(a_high, b_low) + dot(a_low, b_high)


def split(x):
    high = x.astype(BF16)
    low = (x - high.astype(F32)).astype(BF16)
    return high, low


def factor_pair(rows, cols, scale, count):
    inner = dot_high(rows, cols, ((1,), (1,)))
    row_sq = jnp.sum(rows * rows, axis=1, keepdims=True)
    ones = jnp.ones((8, rows.shape[1]), F32)
    col_sq = dot_high(ones, cols * cols, ((1,), (1,)))[0:1, :]
    dist = row_sq + col_sq - 2.0 * inner
    kern = jnp.exp(-dist / (2.0 * scale * scale)) * (1.0 / math.sqrt(count))
    deriv = kern * dist / (scale * scale * scale)
    return kern, deriv


PAIRS = 12


def day_kernel(scales, embed, probe, residual, out, weights):
    step = pl.program_id(0)

    @pl.when(step == 0)
    def _():
        row = lax.broadcasted_iota(jnp.int32, (128, ND), 0)
        day = lax.broadcasted_iota(jnp.int32, (128, ND), 1)
        pick = (day == (row // 8) * 2 + row % 2).astype(F32)
        rows = dot_high(pick, embed[...], ((1,), (1,)))
        col = lax.broadcasted_iota(jnp.int32, (192, ND), 0)
        day = lax.broadcasted_iota(jnp.int32, (192, ND), 1)
        pick = (day == col % ND).astype(F32)
        cols = dot_high(pick, embed[...], ((1,), (1,)))
        kern, deriv = factor_pair(rows, cols, scales[2], ND)
        row = lax.broadcasted_iota(jnp.int32, (128, 192), 0)
        col = lax.broadcasted_iota(jnp.int32, (128, 192), 1)
        both = jnp.where((row // 2) % 2 == 1, deriv, kern)
        high = both.astype(BF16).astype(F32)
        part = jnp.where((col // ND) % 3 == 2, both - high, high)
        weights[...] = jnp.where((row // 4) % 2 == col // 96, part, 0.0).astype(BF16)

    lane = lax.broadcasted_iota(jnp.int32, (ND, 128), 1)
    none = jnp.zeros((ND, 128 - REST), F32)

    def operand(lat):
        one = jnp.concatenate([probe[lat, :, 128:LOCAL_LON], none], axis=1)
        two = jnp.concatenate([residual[lat, :, 128:LOCAL_LON], none], axis=1)
        rest = jnp.where(lane < 64, one, pltpu.roll(two, 64, 1))
        x = jnp.concatenate([probe[lat, :, 0:128], residual[lat, :, 0:128], rest], axis=1)
        x = jnp.where(step * (2 * PAIRS) + lat < LATS, x, 0.0)
        high, low = split(x)
        return [high, low, high]

    for pair in range(PAIRS):
        stacked = jnp.concatenate(operand(2 * pair) + operand(2 * pair + 1), axis=0)
        value = jnp.dot(weights[...], stacked, preferred_element_type=F32)
        for dst in range(16):
            for block in range(3):
                out[dst, pl.ds(pair * 24 + block, 8, stride=3), :] = value[
                    dst * 8 : dst * 8 + 8, block * 128 : block * 128 + 128
                ]


def day_products(scales, embed, probe, residual):
    field = pl.BlockSpec((2 * PAIRS, ND, LOCAL_LON), lambda i: (i, 0, 0))
    return pl.pallas_call(
        day_kernel,
        grid=(pl.cdiv(SLOTS, 2 * PAIRS),),
        out_shape=jax.ShapeDtypeStruct((16, DAY_ROWS, 128), F32),
        in_specs=[
            pl.BlockSpec(memory_space=pltpu.SMEM),
            pl.BlockSpec((16, ND), lambda i: (0, 0)),
            field,
            field,
        ],
        out_specs=pl.BlockSpec((16, 24 * PAIRS, 128), lambda i: (0, i, 0)),
        scratch_shapes=[pltpu.VMEM((128, 192), BF16)],
        compiler_params=params(),
        name="day_products",
    )(scales, embed, probe, residual)


def factor_kernel(which, count, scales, rows, cols, high, low):
    kern, deriv = factor_pair(rows[...], cols[...], scales[which], count)
    for at, value in enumerate((kern, deriv)):
        high[at], low[at] = split(value)


def factor_halves(scales, which, count, rows, cols, held=False):
    nr, nc = rows.shape[0], cols.shape[0]
    shape = (pltpu.VMEM if held else jax.ShapeDtypeStruct)((2, nr, nc), BF16)
    block = pl.BlockSpec((2, 256, nc), lambda i: (0, i, 0))
    return pl.pallas_call(
        functools.partial(factor_kernel, which, count),
        grid=(nr // 256,),
        out_shape=(shape, shape),
        in_specs=[
            pl.BlockSpec(memory_space=pltpu.SMEM),
            pl.BlockSpec((256, 16), lambda i: (i, 0)),
            pl.BlockSpec((nc, 16), lambda i: (0, 0)),
        ],
        out_specs=(block, block),
        compiler_params=params(30),
        cost_estimate=pl.CostEstimate(
            flops=2 * 96 * nr * nc, bytes_accessed=8 * nr * nc, transcendentals=nr * nc
        ),
        name="factors",
    )(scales, rows, cols)


TERM_ROWS = 544


def lat_kernel(kinds, moved, *refs):
    count = len(kinds)
    factors, outs = refs[: 2 * count], refs[2 * count : 10 * count]
    held, sems = refs[10 * count :]
    copies = []
    for at, (op, _) in enumerate(kinds):
        for block in range(3):
            parts = [
                split(moved[pl.ds((op * 2 + day) * 3 + block, 16 * SLOTS, stride=12), :])
                for day in range(2)
            ]
            x_high, x_low = [jnp.concatenate([p[half] for p in parts], axis=1) for half in range(2)]
            value = dot_halves(factors[2 * at][0], factors[2 * at + 1][0], x_high, x_low)
            for step in range(8):
                for day in range(2):
                    held[8 * at + step, pl.ds(block * KIND_ROWS + day, OUT_LATS, stride=2), :] = (
                        value[step * 96 : step * 96 + OUT_LATS, day * 128 : day * 128 + 128]
                    )
        for step in range(8):
            place = 8 * at + step
            copies.append(pltpu.make_async_copy(held.at[place], outs[place], sems.at[place]))
            copies[-1].start()
    for copy in copies:
        copy.wait()


def lat_products(moved, high, low, kinds):
    count = len(kinds)
    in_specs, args = [pl.BlockSpec((16 * DAY_ROWS, 128), lambda i: (0, 0))], [moved]
    for _, which in kinds:
        in_specs += [pl.BlockSpec((1, 768, 16 * SLOTS), lambda i, which=which: (which, 0, 0))] * 2
        args += [pltpu.with_memory_space_constraint(x, pltpu.HBM) for x in (high, low)]
    terms = pl.pallas_call(
        functools.partial(lat_kernel, kinds),
        grid=(1,),
        out_shape=[jax.ShapeDtypeStruct((TERM_ROWS, 128), F32)] * (8 * count),
        in_specs=in_specs,
        out_specs=[pl.BlockSpec(memory_space=pl.ANY)] * (8 * count),
        scratch_shapes=[
            pltpu.VMEM((8 * count, TERM_ROWS, 128), F32),
            pltpu.SemaphoreType.DMA((8 * count,)),
        ],
        compiler_params=params(28),
        cost_estimate=pl.CostEstimate(
            flops=2 * 3 * 768 * 768 * 768 * count, bytes_accessed=10**7, transcendentals=0
        ),
        name="lat_products",
    )(*args)
    return [terms[8 * at : 8 * at + 8] for at in range(count)]


def lay_out(read, put, rows):
    for src in range(8):
        for field in range(2):
            put(field, src, read(src, field))
    first = lax.broadcasted_iota(jnp.int32, (rows, 128), 1) < 64
    for pair in range(4):
        one, two = read(2 * pair, 2), read(2 * pair + 1, 2)
        put(0, 8 + pair, jnp.where(first, one, pltpu.roll(two, 64, 1)))
        put(1, 8 + pair, jnp.where(first, pltpu.roll(one, 64, 1), two))


def by_day(value, start):
    return value[start : start + KIND_ROWS].reshape(OUT_LATS, 2, value.shape[1])


WIDE = 1536
FIELD_ROWS = 192


def lon_kernel(count, *refs):
    terms, (high, low) = refs[:8], refs[8:10]
    out, z_high, z_low = refs[-3:]
    wide = out.shape[-1]
    cols = pl.ds(pl.multiple_of(pl.program_id(0) * wide, wide), wide)

    @pl.when(pl.program_id(0) == 0)
    def _():
        def read(step, block):
            return terms[step][block * KIND_ROWS : block * KIND_ROWS + KIND_ROWS, :]

        def put(field, col, value):
            at = pl.ds(col * 128, 128)
            for z, half in zip((z_high, z_low), split(value)):
                z[field * FIELD_ROWS : field * FIELD_ROWS + KIND_ROWS, at] = half

        lay_out(read, put, KIND_ROWS)

    for at in range(count):
        value = dot_halves(z_high[...], z_low[...], high[at, :, cols], low[at, :, cols])
        for field in range(2):
            out[field, at, 0] = by_day(value, field * FIELD_ROWS)


def lon_products(terms, high, low, operators, so_far=None, wide=512):
    count = len(operators)
    high_at, low_at = divmod(operators[0], 2)
    in_specs = [pl.BlockSpec((TERM_ROWS, 128), lambda n: (0, 0))] * 8
    in_specs += [pl.BlockSpec(memory_space=pltpu.VMEM)] * 2
    args = [*terms] + [pltpu.with_memory_space_constraint(x, pltpu.VMEM) for x in (high, low)]
    aliases = {}
    if so_far is not None:
        aliases = {len(args): 0}
        in_specs.append(pl.BlockSpec(memory_space=pl.ANY))
        args.append(so_far)
    return pl.pallas_call(
        functools.partial(lon_kernel, count),
        grid=(pl.cdiv(NL, wide),),
        out_shape=jax.ShapeDtypeStruct((2, 2, 2, OUT_LATS, 2, NL), F32),
        in_specs=in_specs,
        out_specs=pl.BlockSpec(
            (2, count, 1, OUT_LATS, 2, wide), lambda n: (0, high_at, low_at, 0, 0, n)
        ),
        scratch_shapes=[pltpu.VMEM((2 * FIELD_ROWS, 1536), BF16)] * 2,
        input_output_aliases=aliases,
        compiler_params=params(18),
        cost_estimate=pl.CostEstimate(
            flops=2 * 3 * 360 * 1536 * 1536 * count, bytes_accessed=2 * 10**7, transcendentals=0
        ),
        name="lon_products",
    )(*args)


STEPS = (0, 1, 6, 4, 3, 2, 5, 7)


def local(probe, residual, lon_embed, lat_embed, day_embed, scales):
    sent = day_products(
        scales, day_embed.T, jnp.transpose(probe, (1, 0, 2)), jnp.transpose(residual, (1, 0, 2))
    )
    moved = lax.all_to_all(sent, "lat", split_axis=0, concat_axis=0, tiled=True)
    moved = moved.reshape(16 * DAY_ROWS, 128)

    order = jnp.bitwise_xor(lax.axis_index("lon"), jnp.array(STEPS))
    by_block = lat_embed.reshape(8, OUT_LATS, 16)[order]
    lat_rows = jnp.pad(by_block, ((0, 0), (0, 6), (0, 0))).reshape(768, 16)
    lat_cols = jnp.pad(lat_embed.reshape(16, LATS, 16), ((0, 0), (0, SLOTS - LATS), (0, 0)))
    by_block = lon_embed.reshape(8, LOCAL_LON, 16)[order]
    lon_rest = jnp.pad(by_block[:, 128:], ((0, 0), (0, 64 - REST), (0, 0)))
    lon_rows = jnp.concatenate(
        [by_block[:, :128].reshape(1024, 16), lon_rest.reshape(512, 16)], axis=0
    )
    lat_factors = factor_halves(scales, 1, NA, lat_rows, lat_cols.reshape(16 * SLOTS, 16))
    lon_cols = jnp.pad(lon_embed, ((0, WIDE - NL), (0, 0)))
    lon_factors = factor_halves(scales, 0, NL, lon_rows, lon_cols, held=True)
    moved, lat_factors, lon_factors = lax.optimization_barrier((moved, lat_factors, lon_factors))

    def exchanged(terms):
        return [terms[0]] + [
            lax.ppermute(term, "lon", [(i, i ^ step) for i in range(8)])
            for term, step in zip(terms[1:], STEPS[1:])
        ]

    (by_day,) = lat_products(moved, *lat_factors, ((1, 0),))
    (plain,) = lat_products(moved, *lat_factors, ((0, 0),))
    (by_lat,) = lat_products(moved, *lat_factors, ((0, 1),))
    result = lon_products(exchanged(by_day), *lon_factors, (1,))
    result = lon_products(exchanged(plain), *lon_factors, (0, 2), result)
    result = lon_products(exchanged(by_lat), *lon_factors, (3,), result)
    result = result.reshape(2, 4, OUT_LATS, 2, NL)
    return jnp.transpose(result, (0, 1, 3, 2, 4))


def solution(mesh):
    placed = (P(None, "lat", "lon"), P(None, "lat", "lon"), P(), P(), P(), P())
    return jax.shard_map(
        local,
        mesh=mesh,
        in_specs=placed,
        out_specs=P(None, None, "lat", "lon", None),
        check_vma=False,
    )
```

```python
import functools
import math

import jax
import jax.numpy as jnp
from jax import lax
from jax.experimental import pallas as pl
from jax.experimental.pallas import tpu as pltpu
from jax.sharding import PartitionSpec as P

NL = 1440
NA = 720
ND = 32
F32 = jnp.float32
BF16 = jnp.bfloat16
VMEM_LIMIT = 58 * 1024 * 1024

LOCAL_LON = 180
REST = LOCAL_LON - 128
LATS = 45
SLOTS = 46
DAY_ROWS = SLOTS * 12
OUT_LATS = 90
KIND_ROWS = 2 * OUT_LATS


def params(mib=58):
    return pltpu.CompilerParams(vmem_limit_bytes=mib * 1024 * 1024)


def dot_high(a, b, dims):
    return lax.dot_general(
        a, b, (dims, ((), ())), precision=lax.Precision.HIGHEST, preferred_element_type=F32
    )


def dot_halves(a_high, a_low, b_high, b_low):
    def dot(a, b):
        return jnp.dot(a, b, preferred_element_type=F32)

    return dot(a_high, b_high) + dot(a_high, b_low) + dot(a_low, b_high)


def split(x):
    high = x.astype(BF16)
    low = (x - high.astype(F32)).astype(BF16)
    return high, low


def factor_pair(rows, cols, scale, count):
    inner = dot_high(rows, cols, ((1,), (1,)))
    row_sq = jnp.sum(rows * rows, axis=1, keepdims=True)
    ones = jnp.ones((8, rows.shape[1]), F32)
    col_sq = dot_high(ones, cols * cols, ((1,), (1,)))[0:1, :]
    dist = row_sq + col_sq - 2.0 * inner
    kern = jnp.exp(-dist / (2.0 * scale * scale)) * (1.0 / math.sqrt(count))
    deriv = kern * dist / (scale * scale * scale)
    return kern, deriv


PAIRS = 12


def day_kernel(scales, embed, probe, residual, out, weights):
    step = pl.program_id(0)

    @pl.when(step == 0)
    def _():
        row = lax.broadcasted_iota(jnp.int32, (128, ND), 0)
        day = lax.broadcasted_iota(jnp.int32, (128, ND), 1)
        pick = (day == (row // 8) * 2 + row % 2).astype(F32)
        rows = dot_high(pick, embed[...], ((1,), (1,)))
        col = lax.broadcasted_iota(jnp.int32, (192, ND), 0)
        day = lax.broadcasted_iota(jnp.int32, (192, ND), 1)
        pick = (day == col % ND).astype(F32)
        cols = dot_high(pick, embed[...], ((1,), (1,)))
        kern, deriv = factor_pair(rows, cols, scales[2], ND)
        row = lax.broadcasted_iota(jnp.int32, (128, 192), 0)
        col = lax.broadcasted_iota(jnp.int32, (128, 192), 1)
        both = jnp.where((row // 2) % 2 == 1, deriv, kern)
        high = both.astype(BF16).astype(F32)
        part = jnp.where((col // ND) % 3 == 2, both - high, high)
        weights[...] = jnp.where((row // 4) % 2 == col // 96, part, 0.0).astype(BF16)

    lane = lax.broadcasted_iota(jnp.int32, (ND, 128), 1)
    none = jnp.zeros((ND, 128 - REST), F32)

    def operand(lat):
        one = jnp.concatenate([probe[lat, :, 128:LOCAL_LON], none], axis=1)
        two = jnp.concatenate([residual[lat, :, 128:LOCAL_LON], none], axis=1)
        rest = jnp.where(lane < 64, one, pltpu.roll(two, 64, 1))
        x = jnp.concatenate([probe[lat, :, 0:128], residual[lat, :, 0:128], rest], axis=1)
        x = jnp.where(step * (2 * PAIRS) + lat < LATS, x, 0.0)
        high, low = split(x)
        return [high, low, high]

    for pair in range(PAIRS):
        stacked = jnp.concatenate(operand(2 * pair) + operand(2 * pair + 1), axis=0)
        value = jnp.dot(weights[...], stacked, preferred_element_type=F32)
        for dst in range(16):
            for block in range(3):
                out[dst, pl.ds(pair * 24 + block, 8, stride=3), :] = value[
                    dst * 8 : dst * 8 + 8, block * 128 : block * 128 + 128
                ]


def day_products(scales, embed, probe, residual):
    field = pl.BlockSpec((2 * PAIRS, ND, LOCAL_LON), lambda i: (i, 0, 0))
    return pl.pallas_call(
        day_kernel,
        grid=(pl.cdiv(SLOTS, 2 * PAIRS),),
        out_shape=jax.ShapeDtypeStruct((16, DAY_ROWS, 128), F32),
        in_specs=[
            pl.BlockSpec(memory_space=pltpu.SMEM),
            pl.BlockSpec((16, ND), lambda i: (0, 0)),
            field,
            field,
        ],
        out_specs=pl.BlockSpec((16, 24 * PAIRS, 128), lambda i: (0, i, 0)),
        scratch_shapes=[pltpu.VMEM((128, 192), BF16)],
        compiler_params=params(),
        name="day_products",
    )(scales, embed, probe, residual)


def factor_kernel(which, count, scales, rows, cols, high, low):
    kern, deriv = factor_pair(rows[...], cols[...], scales[which], count)
    for at, value in enumerate((kern, deriv)):
        high[at], low[at] = split(value)


def factor_halves(scales, which, count, rows, cols, held=False):
    nr, nc = rows.shape[0], cols.shape[0]
    shape = (pltpu.VMEM if held else jax.ShapeDtypeStruct)((2, nr, nc), BF16)
    block = pl.BlockSpec((2, 256, nc), lambda i: (0, i, 0))
    return pl.pallas_call(
        functools.partial(factor_kernel, which, count),
        grid=(nr // 256,),
        out_shape=(shape, shape),
        in_specs=[
            pl.BlockSpec(memory_space=pltpu.SMEM),
            pl.BlockSpec((256, 16), lambda i: (i, 0)),
            pl.BlockSpec((nc, 16), lambda i: (0, 0)),
        ],
        out_specs=(block, block),
        compiler_params=params(30),
        cost_estimate=pl.CostEstimate(
            flops=2 * 96 * nr * nc, bytes_accessed=8 * nr * nc, transcendentals=nr * nc
        ),
        name="factors",
    )(scales, rows, cols)


TERM_ROWS = 544


def lat_kernel(kinds, moved, *refs):
    count = len(kinds)
    factors, outs = refs[: 2 * count], refs[2 * count : 10 * count]
    held, sems = refs[10 * count :]
    copies = []
    for at, (op, _) in enumerate(kinds):
        for block in range(3):
            parts = [
                split(moved[pl.ds((op * 2 + day) * 3 + block, 16 * SLOTS, stride=12), :])
                for day in range(2)
            ]
            x_high, x_low = [jnp.concatenate([p[half] for p in parts], axis=1) for half in range(2)]
            value = dot_halves(factors[2 * at][0], factors[2 * at + 1][0], x_high, x_low)
            for step in range(8):
                for day in range(2):
                    held[8 * at + step, pl.ds(block * KIND_ROWS + day, OUT_LATS, stride=2), :] = (
                        value[step * 96 : step * 96 + OUT_LATS, day * 128 : day * 128 + 128]
                    )
        for step in range(8):
            place = 8 * at + step
            copies.append(pltpu.make_async_copy(held.at[place], outs[place], sems.at[place]))
            copies[-1].start()
    for copy in copies:
        copy.wait()


def lat_products(moved, high, low, kinds):
    count = len(kinds)
    in_specs, args = [pl.BlockSpec((16 * DAY_ROWS, 128), lambda i: (0, 0))], [moved]
    for _, which in kinds:
        in_specs += [pl.BlockSpec((1, 768, 16 * SLOTS), lambda i, which=which: (which, 0, 0))] * 2
        args += [pltpu.with_memory_space_constraint(x, pltpu.HBM) for x in (high, low)]
    terms = pl.pallas_call(
        functools.partial(lat_kernel, kinds),
        grid=(1,),
        out_shape=[jax.ShapeDtypeStruct((TERM_ROWS, 128), F32)] * (8 * count),
        in_specs=in_specs,
        out_specs=[pl.BlockSpec(memory_space=pl.ANY)] * (8 * count),
        scratch_shapes=[
            pltpu.VMEM((8 * count, TERM_ROWS, 128), F32),
            pltpu.SemaphoreType.DMA((8 * count,)),
        ],
        compiler_params=params(28),
        cost_estimate=pl.CostEstimate(
            flops=2 * 3 * 768 * 768 * 768 * count, bytes_accessed=10**7, transcendentals=0
        ),
        name="lat_products",
    )(*args)
    return [terms[8 * at : 8 * at + 8] for at in range(count)]


def lay_out(read, put, rows):
    for src in range(8):
        for field in range(2):
            put(field, src, read(src, field))
    first = lax.broadcasted_iota(jnp.int32, (rows, 128), 1) < 64
    for pair in range(4):
        one, two = read(2 * pair, 2), read(2 * pair + 1, 2)
        put(0, 8 + pair, jnp.where(first, one, pltpu.roll(two, 64, 1)))
        put(1, 8 + pair, jnp.where(first, pltpu.roll(one, 64, 1), two))


def by_day(value, start):
    return value[start : start + KIND_ROWS].reshape(OUT_LATS, 2, value.shape[1])


WIDE = 1536
FIELD_ROWS = 192


def lon_kernel(count, order, *refs):
    terms, (high, low) = [refs[order.index(at)] for at in range(8)], refs[8:10]
    out, z_high, z_low = refs[-3:]
    wide = out.shape[-1]
    cols = pl.ds(pl.multiple_of(pl.program_id(0) * wide, wide), wide)

    @pl.when(pl.program_id(0) == 0)
    def _():
        def read(step, block):
            return terms[step][block * KIND_ROWS : block * KIND_ROWS + KIND_ROWS, :]

        def put(field, col, value):
            at = pl.ds(col * 128, 128)
            for z, half in zip((z_high, z_low), split(value)):
                z[field * FIELD_ROWS : field * FIELD_ROWS + KIND_ROWS, at] = half

        lay_out(read, put, KIND_ROWS)

    for at in range(count):
        value = dot_halves(z_high[...], z_low[...], high[at, :, cols], low[at, :, cols])
        for field in range(2):
            out[field, at, 0] = by_day(value, field * FIELD_ROWS)


def lon_products(terms, high, low, operators, so_far=None, wide=512, order=tuple(range(8))):
    count = len(operators)
    high_at, low_at = divmod(operators[0], 2)
    in_specs = [pl.BlockSpec((TERM_ROWS, 128), lambda n: (0, 0))] * 8
    in_specs += [pl.BlockSpec(memory_space=pltpu.VMEM)] * 2
    args = [terms[at] for at in order] + [pltpu.with_memory_space_constraint(x, pltpu.VMEM) for x in (high, low)]
    aliases = {}
    if so_far is not None:
        aliases = {len(args): 0}
        in_specs.append(pl.BlockSpec(memory_space=pl.ANY))
        args.append(so_far)
    return pl.pallas_call(
        functools.partial(lon_kernel, count, order),
        grid=(pl.cdiv(NL, wide),),
        out_shape=jax.ShapeDtypeStruct((2, 2, 2, OUT_LATS, 2, NL), F32),
        in_specs=in_specs,
        out_specs=pl.BlockSpec(
            (2, count, 1, OUT_LATS, 2, wide), lambda n: (0, high_at, low_at, 0, 0, n)
        ),
        scratch_shapes=[pltpu.VMEM((2 * FIELD_ROWS, 1536), BF16)] * 2,
        input_output_aliases=aliases,
        compiler_params=params(18),
        cost_estimate=pl.CostEstimate(
            flops=2 * 3 * 360 * 1536 * 1536 * count, bytes_accessed=2 * 10**7, transcendentals=0
        ),
        name="lon_products",
    )(*args)


STEPS = (0, 1, 6, 4, 3, 2, 5, 7)


def local(probe, residual, lon_embed, lat_embed, day_embed, scales):
    sent = day_products(
        scales, day_embed.T, jnp.transpose(probe, (1, 0, 2)), jnp.transpose(residual, (1, 0, 2))
    )
    moved = lax.all_to_all(sent, "lat", split_axis=0, concat_axis=0, tiled=True)
    moved = moved.reshape(16 * DAY_ROWS, 128)

    order = jnp.bitwise_xor(lax.axis_index("lon"), jnp.array(STEPS))
    by_block = lat_embed.reshape(8, OUT_LATS, 16)[order]
    lat_rows = jnp.pad(by_block, ((0, 0), (0, 6), (0, 0))).reshape(768, 16)
    lat_cols = jnp.pad(lat_embed.reshape(16, LATS, 16), ((0, 0), (0, SLOTS - LATS), (0, 0)))
    by_block = lon_embed.reshape(8, LOCAL_LON, 16)[order]
    lon_rest = jnp.pad(by_block[:, 128:], ((0, 0), (0, 64 - REST), (0, 0)))
    lon_rows = jnp.concatenate(
        [by_block[:, :128].reshape(1024, 16), lon_rest.reshape(512, 16)], axis=0
    )
    lat_factors = factor_halves(scales, 1, NA, lat_rows, lat_cols.reshape(16 * SLOTS, 16))
    lon_cols = jnp.pad(lon_embed, ((0, WIDE - NL), (0, 0)))
    lon_factors = factor_halves(scales, 0, NL, lon_rows, lon_cols, held=True)
    moved, lat_factors, lon_factors = lax.optimization_barrier((moved, lat_factors, lon_factors))

    def exchanged(terms):
        return [terms[0]] + [
            lax.ppermute(term, "lon", [(i, i ^ step) for i in range(8)])
            for term, step in zip(terms[1:], STEPS[1:])
        ]

    (by_day,) = lat_products(moved, *lat_factors, ((1, 0),))
    (plain,) = lat_products(moved, *lat_factors, ((0, 0),))
    (by_lat,) = lat_products(moved, *lat_factors, ((0, 1),))
    result = lon_products(exchanged(by_day), *lon_factors, (1,))
    result = lon_products(exchanged(plain), *lon_factors, (0, 2), result)
    result = lon_products(
        exchanged(by_lat), *lon_factors, (3,), result, order=(0, 1, 2, 3, 6, 7, 4, 5)
    )
    result = result.reshape(2, 4, OUT_LATS, 2, NL)
    return jnp.transpose(result, (0, 1, 3, 2, 4))


def solution(mesh):
    placed = (P(None, "lat", "lon"), P(None, "lat", "lon"), P(), P(), P(), P())
    return jax.shard_map(
        local,
        mesh=mesh,
        in_specs=placed,
        out_specs=P(None, None, "lat", "lon", None),
        check_vma=False,
    )
```
